32 devices in a mesh: freq: 2 (over core), tile: 16 (over z, y, x).
Axes of the slice: x: 2, y: 2, z: 4, core: 2. Of those that a mesh axis runs over, the one named last changes fastest.
Arguments:
- wave_in: bfloat16 [2, 4096, 2, 256], P(None, 'tile', None, 'freq'), may hold values from -6 to 6
- column_basis: bfloat16 [2, 32, 16, 256, 128], P('freq', None, 'tile'), may hold values from -0.25 to 0.25
- row_basis: bfloat16 [2, 32, 16, 256, 128], P('freq', 'tile'), may hold values from -0.1875 to 0.1875
- tile_scale: float32 [2, 32, 16], P('freq'), may hold values from 0.5 to 2
- tile_ranks: int32 [2, 32, 16], P('freq'), may hold values from 16 to 64, as said below
Outputs:
- forward_out: bfloat16 [2, 8192, 2, 256], P('freq', 'tile')
- adjoint_out: bfloat16 [2, 4096, 2, 256], P(None, 'tile', None, 'freq')
The draws below stay inside these ranges and needn't reach their ends.
Inputs may be any that keep to these rules, and one draw needn't show every extreme that they name: `tile_ranks`: every entry is a multiple of 16. For each frequency, in each aligned group of 2 tile rows and 1 tile columns the ranks add up to at most 80, and some group reaches that sum.
All inputs are finite; a program needn't handle non-finite values.
Results may differ from the reference program's by a relative error of at most 0.005.
Values may be sent and summed in bfloat16 or wider, within the bound.
No kernel may reach another device: no remote copies, remote signals or barrier semaphores. Data moves between devices by JAX's collectives and lax.ppermute only.
A program may use at most 192 MiB of HBM per device.

```python
import math
import jax
import jax.numpy as jnp
from jax import lax

NB = 256
RMAX = 64
MT_DEV = 2
NT_DEV = 1
NVS = 256
NF = 2
MT = 32
NT = 16
N = 4096
CAP = 5


def draw_tile_ranks(key, part):
    blocks_max = RMAX // 16
    group_rows = MT // MT_DEV
    group_cols = NT // NT_DEV
    key_total, key_split = jax.random.split(jax.random.fold_in(key, 7))
    extra_blocks = jax.random.randint(key_total, (NF, group_rows, group_cols), 0, CAP - 1)
    group_total = (extra_blocks + 2).at[0, 0, 0].set(CAP)
    lowest = jnp.maximum(1, group_total - blocks_max)
    highest = jnp.minimum(blocks_max, group_total - 1)
    spread = jax.random.randint(key_split, (NF, group_rows, group_cols), 0, 1048576)
    first_blocks = lowest + spread % (highest - lowest + 1)
    first_blocks = first_blocks.at[0, 0, 0].set(blocks_max)
    second = group_total - first_blocks
    paired = jnp.stack([first_blocks, second], -1).reshape(NF, group_rows, group_cols, MT_DEV, NT_DEV)
    paired = jnp.transpose(paired, (0, 1, 3, 2, 4)).reshape(NF, MT, NT)
    return (16 * paired).astype(jnp.int32)


def shard_levels(own_key, shape, shards, least, largest):
    level = 1.0
    for axis_at, parts in shards:
        steps = jax.random.uniform(jax.random.fold_in(jax.random.fold_in(own_key, 6), axis_at), (parts,), jnp.float32, least / len(shards), largest / len(shards))
        level = level * jnp.repeat(jnp.exp(steps), shape[axis_at] // parts).reshape((-1,) + (1,) * (len(shape) - 1 - axis_at))
    return level


def normal_values(rng, dims, scale, reach, cuts=(), kind=jnp.bfloat16):
    gain = shard_levels(rng, dims, cuts, -0.22, 0.18) if cuts else 1.0
    values = jax.random.normal(rng, dims, jnp.float32) * scale * gain
    return jnp.minimum(jnp.maximum(values, -reach), reach).astype(kind)


def setup_inputs(seed: int = 0) -> dict:
    seeds = jax.random.split(jax.random.key(seed), 6)
    wave_in = normal_values(seeds[0], (NF, N, 2, NVS), 1.0, 6.0, ((1, 16), (3, 2)))
    column_basis = normal_values(seeds[1], (NF, MT, NT, NB, 2 * RMAX), (2 * NB) ** -0.5, 0.25, ((0, 2), (2, 16)))
    row_basis = normal_values(seeds[2], (NF, MT, NT, NB, 2 * RMAX), (NT * RMAX) ** -0.5, 0.1875, ((0, 2), (1, 16)))
    tile_scale = jnp.clip(jnp.exp(math.log(2.0) - 1.3862944 * jax.random.uniform(seeds[3], (NF, MT, NT), jnp.float32) ** shard_levels(seeds[3], (NF, MT, NT), ((0, 2),), -0.2, 0.2)), 0.5, 2.0)
    tile_ranks = draw_tile_ranks(jax.random.fold_in(seeds[5], 71), 0)
    return {"wave_in": wave_in, "column_basis": column_basis, "row_basis": row_basis, "tile_scale": tile_scale, "tile_ranks": tile_ranks}


def combine_conj(products):
    shaped = products.reshape(products.shape[:-3] + (products.shape[-3] // 32, 2, 16) + products.shape[-2:])
    real_part = shaped[..., 0, :, 0, :] + shaped[..., 1, :, 1, :]
    imag_part = shaped[..., 0, :, 1, :] - shaped[..., 1, :, 0, :]
    return jnp.stack([real_part, imag_part], -3)


def combine_plain(summed):
    real_part = summed[..., 0, 0, :] - summed[..., 1, 1, :]
    imag_part = summed[..., 0, 1, :] + summed[..., 1, 0, :]
    return jnp.stack([real_part, imag_part], -2)


def reference(wave_in, column_basis, row_basis, tile_scale, tile_ranks):
    blocks = RMAX // 16
    forward_list = []
    adjoint_list = []
    for freq_index in range(NF):
        wavefield = wave_in[freq_index].reshape(NT, NB, 2, NVS).astype(jnp.float32)
        live_mask = ((16 * jnp.arange(blocks, dtype=jnp.int32))[None, None, :] < tile_ranks[freq_index][:, :, None]).astype(jnp.float32)
        weights = tile_scale[freq_index][:, :, None] * live_mask
        column_bases = column_basis[freq_index]
        row_bases = row_basis[freq_index]

        def forward_step(running, column):
            column_tile = column_bases[:, column].astype(jnp.float32)
            products = jnp.einsum("mbc,bpn->mcpn", column_tile, wavefield[column], precision=lax.Precision.HIGHEST)
            coded_rows = combine_conj(products) * weights[:, column][:, :, None, None, None]
            coded_rows = lax.optimization_barrier(coded_rows.astype(jnp.bfloat16)).astype(jnp.float32)
            row_tile = row_bases[:, column].astype(jnp.float32).reshape(MT, NB, blocks, 2, 16)
            summed = jnp.einsum("mbkqt,mkptn->mbqpn", row_tile, coded_rows, precision=lax.Precision.HIGHEST)
            return running + combine_plain(summed), None

        start_sum = jnp.zeros((MT, NB, 2, NVS), jnp.float32)
        forward_sum, _ = lax.scan(forward_step, start_sum, jnp.arange(NT, dtype=jnp.int32))
        forward = lax.optimization_barrier(forward_sum.astype(jnp.bfloat16))
        forward_wide = forward.astype(jnp.float32)

        def adjoint_step(running, row_index):
            row_tile = row_bases[row_index].astype(jnp.float32)
            products = jnp.einsum("jbc,bpn->jcpn", row_tile, forward_wide[row_index], precision=lax.Precision.HIGHEST)
            returned = combine_conj(products) * weights[row_index][:, :, None, None, None]
            returned = lax.optimization_barrier(returned.astype(jnp.bfloat16)).astype(jnp.float32)
            column_tile = column_bases[row_index].astype(jnp.float32).reshape(NT, NB, blocks, 2, 16)
            summed = jnp.einsum("jbkqt,jkptn->jbqpn", column_tile, returned, precision=lax.Precision.HIGHEST)
            return running + combine_plain(summed), None

        start_adj = jnp.zeros((NT, NB, 2, NVS), jnp.float32)
        adjoint_sum, _ = lax.scan(adjoint_step, start_adj, jnp.arange(MT, dtype=jnp.int32))
        forward_list.append(forward.reshape(MT * NB, 2, NVS))
        adjoint_list.append(adjoint_sum.astype(jnp.bfloat16).reshape(NT * NB, 2, NVS))
    return jnp.stack(forward_list), jnp.stack(adjoint_list)
```

```python
import jax
import jax.numpy as jnp
from jax import lax
from jax.experimental import pallas as pl
from jax.experimental.pallas import tpu as pltpu
from jax.sharding import PartitionSpec as P

CAP = 5
RB = 16
VMEM = pl.BlockSpec(memory_space=pltpu.VMEM)
SMEM = pl.BlockSpec(memory_space=pltpu.SMEM)


def params():
    return pltpu.CompilerParams(vmem_limit_bytes=32 * 1024 * 1024)


def code_tiles(bases, waves, scales, first_blocks, store):
    coded = []
    for base, wave, scale in zip(bases, waves, scales):
        product = lax.dot_general(
            base, wave, (((0,), (0,)), ((), ())), preferred_element_type=jnp.float32
        )
        n = product.shape[1] // 2
        blocks = []
        for k in range(product.shape[0] // (2 * RB)):
            top = product[2 * RB * k : 2 * RB * k + RB]
            low = product[2 * RB * k + RB : 2 * RB * (k + 1)]
            both = jnp.concatenate([top[:, :n] + low[:, n:], top[:, n:] - low[:, :n]], 0)
            blocks.append((both * scale).astype(jnp.bfloat16))
        coded.append(blocks)
    for k, block in enumerate(coded[0]):
        store(min(k, CAP - 1), block)
    for k in reversed(range(len(coded[1]))):
        store(jnp.minimum(first_blocks + k, CAP - 1), coded[1][k])


def open_slots(load, counts, tile, blocks):
    rows = []
    for k in range(blocks):
        slot = min(k, CAP - 1) if tile == 0 else jnp.minimum(counts[0] + k, CAP - 1)
        block = load(slot)
        block = jnp.where(k < counts[tile], block, jnp.zeros_like(block))
        real, imag = block[:RB], block[RB:]
        rows.append(jnp.concatenate([real, imag], 1))
        rows.append(jnp.concatenate([-imag, real], 1))
    return jnp.concatenate(rows, 0)


def counts_of(ranks_ref, group, column):
    return ranks_ref[2 * group, column] // RB, ranks_ref[2 * group + 1, column] // RB


def coded_kernel(tiles, me_ref, ranks_ref, scale_ref, v_ref, x_ref, out_ref):
    me = me_ref[0]

    def step(r, carry):
        group = r
        first, _ = counts_of(ranks_ref, group, me)

        def store(slot, block):
            out_ref[r, slot] = block

        wave = x_ref[...]
        code_tiles(
            [v_ref[2 * group], v_ref[2 * group + 1]],
            [wave, wave],
            [scale_ref[2 * group, me], scale_ref[2 * group + 1, me]],
            first,
            store,
        )
        return carry

    lax.fori_loop(0, tiles, step, 0, unroll=4)


def middle_kernel(tiles, me_ref, ranks_ref, scale_ref, u_ref, in_ref, y_ref, out_ref, rhs):
    me = me_ref[0]
    blocks = u_ref.shape[3] // (2 * RB)
    depth = u_ref.shape[3]

    def unpack(r, carry):
        counts = counts_of(ranks_ref, me, r)
        for tile in range(2):
            rhs[tile, r] = open_slots(lambda slot: in_ref[r, slot], counts, tile, blocks)
        return carry

    lax.fori_loop(0, tiles, unpack, 0, unroll=2)
    for tile in range(2):

        def add(pair, total):
            left = jnp.concatenate([u_ref[tile, 2 * pair], u_ref[tile, 2 * pair + 1]], 1)
            right = jnp.concatenate([rhs[tile, 2 * pair], rhs[tile, 2 * pair + 1]], 0)
            return total + jnp.dot(left, right, preferred_element_type=jnp.float32)

        total = jnp.zeros(y_ref.shape[1:], jnp.float32)
        y_ref[tile] = lax.fori_loop(0, tiles // 2, add, total, unroll=8).astype(jnp.bfloat16)

    def back(r, carry):
        first, _ = counts_of(ranks_ref, me, r)

        def store(slot, block):
            out_ref[r, slot] = block

        code_tiles(
            [u_ref[0, r], u_ref[1, r]],
            [y_ref[0], y_ref[1]],
            [scale_ref[2 * me, r], scale_ref[2 * me + 1, r]],
            first,
            store,
        )
        return carry

    lax.fori_loop(0, tiles, back, 0, unroll=4)


def adjoint_kernel(tiles, me_ref, ranks_ref, v_ref, in_ref, z_ref):
    me = me_ref[0]
    blocks = v_ref.shape[2] // (2 * RB)

    def add(r, total):
        counts = counts_of(ranks_ref, r, me)
        right = jnp.concatenate(
            [open_slots(lambda slot: in_ref[r, slot], counts, t, blocks) for t in range(2)], 0
        )
        left = jnp.concatenate([v_ref[2 * r], v_ref[2 * r + 1]], 1)
        return total + jnp.dot(left, right, preferred_element_type=jnp.float32)

    total = lax.fori_loop(0, tiles, add, jnp.zeros(z_ref.shape, jnp.float32), unroll=4)
    z_ref[...] = total.astype(jnp.bfloat16)


def per_device(wave_in, column_basis, row_basis, tile_scale, tile_ranks):
    tiles = lax.axis_size("tile")
    core = lax.axis_index("freq")
    me = lax.axis_index("tile").astype(jnp.int32).reshape(1)
    v, u = column_basis[0].reshape(column_basis.shape[1], *column_basis.shape[3:]), row_basis[0]
    scales, ranks = tile_scale[0], tile_ranks[0]
    height, width, depth = v.shape[1], v.shape[2], 2 * RB
    half = wave_in.shape[3]
    n = 2 * half

    swap = [(0, 1), (1, 0)]
    mine = lax.dynamic_index_in_dim(wave_in, core, 0, keepdims=False)
    theirs = lax.dynamic_index_in_dim(wave_in, 1 - core, 0, keepdims=False)
    other = lax.ppermute(theirs, "freq", swap)
    x = jnp.concatenate([mine, other], 2).reshape(height, 2 * n)

    def send(blocks):
        return lax.all_to_all(blocks, "tile", split_axis=0, concat_axis=0, tiled=True)

    slots = jax.ShapeDtypeStruct((tiles, CAP, depth, n), jnp.bfloat16)
    coded = pl.pallas_call(
        lambda *refs: coded_kernel(tiles, *refs),
        out_shape=slots,
        in_specs=[SMEM, SMEM, SMEM, VMEM, VMEM],
        out_specs=VMEM,
        compiler_params=params(),
    )(me, ranks, scales, v, x)
    y, back = pl.pallas_call(
        lambda *refs: middle_kernel(tiles, *refs),
        out_shape=(jax.ShapeDtypeStruct((2, height, 2 * n), jnp.bfloat16), slots),
        in_specs=[SMEM, SMEM, SMEM, VMEM, VMEM],
        out_specs=(VMEM, VMEM),
        scratch_shapes=[pltpu.VMEM((2, tiles, width, 2 * n), jnp.bfloat16)],
        compiler_params=params(),
    )(me, ranks, scales, u, send(coded))
    z = pl.pallas_call(
        lambda *refs: adjoint_kernel(tiles, *refs),
        out_shape=jax.ShapeDtypeStruct((height, 2 * n), jnp.bfloat16),
        in_specs=[SMEM, SMEM, VMEM, VMEM],
        out_specs=VMEM,
        compiler_params=params(),
    )(me, ranks, v, send(back))

    def in_order(first, second):
        return jnp.where(core == 0, first, second), jnp.where(core == 0, second, first)

    y = y.reshape(2 * height, 2, n)
    forward_out = jnp.concatenate(in_order(y[:, :, :half], y[:, :, half:]), 2)[None]
    z = z.reshape(height, 2, n)
    adjoint_out = jnp.stack(in_order(z[:, :, :half], lax.ppermute(z[:, :, half:], "freq", swap)))
    return forward_out, adjoint_out


def solution(mesh):
    return jax.shard_map(
        per_device,
        mesh=mesh,
        in_specs=(
            P(None, "tile", None, "freq"),
            P("freq", None, "tile", None, None),
            P("freq", "tile", None, None, None),
            P("freq", None, None),
            P("freq", None, None),
        ),
        out_specs=(P("freq", "tile", None, None), P(None, "tile", None, "freq")),
        check_vma=False,
    )
```

```python
import jax
import jax.numpy as jnp
from jax import lax
from jax.experimental import pallas as pl
from jax.experimental.pallas import tpu as pltpu
from jax.sharding import PartitionSpec as P

CAP = 5
RB = 16
VMEM = pl.BlockSpec(memory_space=pltpu.VMEM)
SMEM = pl.BlockSpec(memory_space=pltpu.SMEM)


def params():
    return pltpu.CompilerParams(vmem_limit_bytes=32 * 1024 * 1024)


def code_tiles(bases, waves, scales, first_blocks, store):
    coded = []
    for base, wave, scale in zip(bases, waves, scales):
        product = lax.dot_general(
            base, wave, (((0,), (0,)), ((), ())), preferred_element_type=jnp.float32
        )
        n = product.shape[1] // 2
        blocks = []
        for k in range(product.shape[0] // (2 * RB)):
            top = product[2 * RB * k : 2 * RB * k + RB]
            low = product[2 * RB * k + RB : 2 * RB * (k + 1)]
            both = jnp.concatenate([top[:, :n] + low[:, n:], top[:, n:] - low[:, :n]], 0)
            blocks.append((both * scale).astype(jnp.bfloat16))
        coded.append(blocks)
    for k, block in enumerate(coded[0]):
        store(min(k, CAP - 1), block)
    for k in reversed(range(len(coded[1]))):
        store(jnp.minimum(first_blocks + k, CAP - 1), coded[1][k])


def open_slots(load, counts, tile, blocks):
    rows = []
    for k in range(blocks):
        slot = min(k, CAP - 1) if tile == 0 else jnp.minimum(counts[0] + k, CAP - 1)
        block = load(slot)
        block = jnp.where(k < counts[tile], block, jnp.zeros_like(block))
        real, imag = block[:RB], block[RB:]
        rows.append(jnp.concatenate([real, imag], 1))
        rows.append(jnp.concatenate([-imag, real], 1))
    return jnp.concatenate(rows, 0)


def counts_of(ranks_ref, group, column):
    return ranks_ref[2 * group, column] // RB, ranks_ref[2 * group + 1, column] // RB


def far_first(tiles):
    bits = tiles.bit_length() - 1
    low, high = 2 ** (bits // 2), 2 ** (bits - bits // 2)
    return high, low, low, 1


def near_first(tiles):
    count_a, s1, count_b, s2 = far_first(tiles)
    return count_b, s2, count_a, s1


def at_once(tiles):
    return None


def exchange(blocks, route, tiles):
    if route is None:
        return [lax.all_to_all(blocks[0], "tile", split_axis=0, concat_axis=0, tiled=True)]
    count_a, s1, count_b, s2 = route

    def swap(block, offset):
        return lax.ppermute(block, "tile", [(i, i ^ offset) for i in range(tiles)])

    hops = {a: swap(blocks[a], a * s1) for a in reversed(range(1, count_a))}
    first = [blocks[0]] + [hops[a] for a in range(1, count_a)]
    hops = {
        b: swap(jnp.stack([first[a][b] for a in range(count_a)]), b * s2)
        for b in reversed(range(1, count_b))
    }
    return first + [hops[b] for b in range(1, count_b)]


def shapes_sent(route, tiles, shape):
    if route is None:
        return [jax.ShapeDtypeStruct((tiles,) + shape, jnp.bfloat16)]
    return [jax.ShapeDtypeStruct((route[2],) + shape, jnp.bfloat16)] * route[0]


def n_arrays(route):
    return 1 if route is None else route[0] + route[2] - 1


def each_arrival(route, me, refs, visit):
    if route is None:

        def direct(i, carry):
            visit(i, lambda slot: refs[0][i, slot])
            return carry

        lax.fori_loop(0, refs[0].shape[0], direct, 0, unroll=4)
        return
    count_a, s1, count_b, s2 = route
    for a in range(count_a):
        visit(me ^ (a * s1), lambda slot, a=a: refs[a][0, slot])
    for b in range(1, count_b):
        ref = refs[count_a + b - 1]

        def step(a, carry, ref=ref, b=b):
            visit(me ^ (a * s1) ^ (b * s2), lambda slot: ref[a, slot])
            return carry

        lax.fori_loop(0, count_a, step, 0, unroll=4)


def each_departure(route, me, refs, visit):
    for a, ref in enumerate(refs):

        def step(b, carry, ref=ref, a=a):
            def store(slot, block):
                ref[b, slot] = block

            visit(b if route is None else me ^ (a * route[1]) ^ (b * route[3]), store)
            return carry

        lax.fori_loop(0, ref.shape[0], step, 0, unroll=4)


def coded_kernel(route, me_ref, ranks_ref, scale_ref, v_ref, x_ref, *out_refs):
    me = me_ref[0]

    def visit(group, store):
        first, _ = counts_of(ranks_ref, group, me)
        wave = x_ref[...]
        code_tiles(
            [v_ref[2 * group], v_ref[2 * group + 1]],
            [wave, wave],
            [scale_ref[2 * group, me], scale_ref[2 * group + 1, me]],
            first,
            store,
        )

    each_departure(route, me, out_refs, visit)


def middle_kernel(route_in, route_out, tiles, *refs):
    me_ref, ranks_ref, scale_ref, u_ref = refs[:4]
    in_refs, y_ref, out_refs, rhs = (
        refs[4 : 4 + n_arrays(route_in)],
        refs[4 + n_arrays(route_in)],
        refs[5 + n_arrays(route_in) : -1],
        refs[-1],
    )
    me = me_ref[0]
    blocks = u_ref.shape[3] // (2 * RB)

    def unpack(column, load):
        counts = counts_of(ranks_ref, me, column)
        for tile in range(2):
            rhs[tile, column] = open_slots(load, counts, tile, blocks)

    each_arrival(route_in, me, in_refs, unpack)
    for tile in range(2):

        def add(pair, total):
            left = jnp.concatenate([u_ref[tile, 2 * pair], u_ref[tile, 2 * pair + 1]], 1)
            right = jnp.concatenate([rhs[tile, 2 * pair], rhs[tile, 2 * pair + 1]], 0)
            return total + jnp.dot(left, right, preferred_element_type=jnp.float32)

        total = jnp.zeros(y_ref.shape[1:], jnp.float32)
        y_ref[tile] = lax.fori_loop(0, tiles // 2, add, total, unroll=8).astype(jnp.bfloat16)

    def visit(column, store):
        first, _ = counts_of(ranks_ref, me, column)
        code_tiles(
            [u_ref[0, column], u_ref[1, column]],
            [y_ref[0], y_ref[1]],
            [scale_ref[2 * me, column], scale_ref[2 * me + 1, column]],
            first,
            store,
        )

    each_departure(route_out, me, out_refs, visit)


def adjoint_kernel(route, tiles, *refs):
    me_ref, ranks_ref, v_ref, in_refs, z_ref, rhs = *refs[:3], refs[3:-2], *refs[-2:]
    me = me_ref[0]
    blocks = v_ref.shape[2] // (2 * RB)

    def unpack(group, load):
        counts = counts_of(ranks_ref, group, me)
        rhs[group] = jnp.concatenate([open_slots(load, counts, t, blocks) for t in range(2)], 0)

    each_arrival(route, me, in_refs, unpack)

    def add(group, total):
        left = jnp.concatenate([v_ref[2 * group], v_ref[2 * group + 1]], 1)
        return total + jnp.dot(left, rhs[group], preferred_element_type=jnp.float32)

    total = lax.fori_loop(0, tiles, add, jnp.zeros(z_ref.shape, jnp.float32), unroll=8)
    z_ref[...] = total.astype(jnp.bfloat16)


def order_rows_kernel(core_ref, first_ref, second_ref, out_ref):
    n = first_ref.shape[1] // 2
    swapped = core_ref[0] == 1
    first, second = first_ref[...], second_ref[...]
    low = jnp.where(swapped, second, first)
    high = jnp.where(swapped, first, second)
    out_ref[:, 0 * n : 1 * n] = low[:, :n]
    out_ref[:, 1 * n : 2 * n] = high[:, :n]
    out_ref[:, 2 * n : 3 * n] = low[:, n:]
    out_ref[:, 3 * n : 4 * n] = high[:, n:]


def order_parts_kernel(core_ref, first_ref, second_ref, out_ref):
    out_ref[core_ref[0]] = first_ref[...]
    out_ref[1 - core_ref[0]] = second_ref[...]


WAYS = {"1a": far_first, "1b": near_first, "2a": far_first, "2b": near_first}


def per_device(wave_in, column_basis, row_basis, tile_scale, tile_ranks):
    tiles = lax.axis_size("tile")
    core = lax.axis_index("freq").astype(jnp.int32)
    core_at = core.reshape(1)
    me = lax.axis_index("tile").astype(jnp.int32).reshape(1)
    v = column_basis.reshape(column_basis.shape[1], *column_basis.shape[3:])
    u = row_basis[0]
    scales, ranks = tile_scale[0], tile_ranks[0]
    height, width = v.shape[1], v.shape[2]
    n = wave_in.shape[3]
    slots = (CAP, 2 * RB, n)
    swap = [(0, 1), (1, 0)]
    way = {name: pick(tiles) for name, pick in WAYS.items()}

    def cost(products, operands):
        return pl.CostEstimate(
            flops=4 * products * tiles * height * width * 2 * n,
            bytes_accessed=sum(a.size * a.dtype.itemsize for a in operands),
            transcendentals=0,
        )

    def code(x, route):
        shapes = shapes_sent(route, tiles, slots)
        return pl.pallas_call(
            lambda *refs: coded_kernel(route, *refs),
            out_shape=shapes,
            in_specs=[SMEM, SMEM, SMEM, VMEM, VMEM],
            out_specs=[VMEM] * len(shapes),
            compiler_params=params(),
            cost_estimate=cost(1, [v, x]),
        )(me, ranks, scales, v, x)

    def middle(arrived, route_in, route_out):
        shapes = shapes_sent(route_out, tiles, slots)
        result = pl.pallas_call(
            lambda *refs: middle_kernel(route_in, route_out, tiles, *refs),
            out_shape=[jax.ShapeDtypeStruct((2, height, 2 * n), jnp.bfloat16)] + shapes,
            in_specs=[SMEM, SMEM, SMEM, VMEM] + [VMEM] * len(arrived),
            out_specs=[VMEM] * (1 + len(shapes)),
            scratch_shapes=[pltpu.VMEM((2, tiles, width, 2 * n), jnp.bfloat16)],
            compiler_params=params(),
            cost_estimate=cost(2, [u, *arrived]),
        )(me, ranks, scales, u, *arrived)
        return result[0].reshape(2 * height, 2 * n), result[1:]

    def adjoint(arrived, route):
        return pl.pallas_call(
            lambda *refs: adjoint_kernel(route, tiles, *refs),
            out_shape=jax.ShapeDtypeStruct((height, 2 * n), jnp.bfloat16),
            in_specs=[SMEM, SMEM, VMEM] + [VMEM] * len(arrived),
            out_specs=VMEM,
            scratch_shapes=[pltpu.VMEM((tiles, 2 * width, 2 * n), jnp.bfloat16)],
            compiler_params=params(),
            cost_estimate=cost(1, [v, *arrived]),
        )(me, ranks, v, *arrived)

    def ordered(kernel, first, second, shape):
        return pl.pallas_call(
            kernel,
            out_shape=jax.ShapeDtypeStruct(shape, jnp.bfloat16),
            in_specs=[SMEM, VMEM, VMEM],
            out_specs=VMEM,
            compiler_params=params(),
        )(core_at, first, second)

    theirs = lax.dynamic_index_in_dim(wave_in, 1 - core, 0, keepdims=False)
    mine = lax.dynamic_index_in_dim(wave_in, core, 0, keepdims=False)
    other = lax.ppermute(theirs, "freq", swap)
    coded_a = exchange(code(mine.reshape(height, 2 * n), way["1a"]), way["1a"], tiles)
    coded_b = exchange(code(other.reshape(height, 2 * n), way["1b"]), way["1b"], tiles)
    y_a, back_a = middle(coded_a, way["1a"], way["2a"])
    back_a = exchange(back_a, way["2a"], tiles)
    y_b, back_b = middle(coded_b, way["1b"], way["2b"])
    back_b = exchange(back_b, way["2b"], tiles)
    z_a = adjoint(back_a, way["2a"])
    z_b = lax.ppermute(adjoint(back_b, way["2b"]), "freq", swap)
    forward_out = ordered(order_rows_kernel, y_a, y_b, (2 * height, 4 * n))
    adjoint_out = ordered(order_parts_kernel, z_a, z_b, (2, height, 2 * n))
    return forward_out.reshape(1, 2 * height, 2, 2 * n), adjoint_out.reshape(2, height, 2, n)


def solution(mesh):
    return jax.shard_map(
        per_device,
        mesh=mesh,
        in_specs=(
            P(None, "tile", None, "freq"),
            P("freq", None, "tile", None, None),
            P("freq", "tile", None, None, None),
            P("freq", None, None),
            P("freq", None, None),
        ),
        out_specs=(P("freq", "tile", None, None), P(None, "tile", None, "freq")),
        check_vma=False,
    )
```

```python
import jax
import jax.numpy as jnp
from jax import lax
from jax.experimental import pallas as pl
from jax.experimental.pallas import tpu as pltpu
from jax.sharding import PartitionSpec as P

CAP = 5
RB = 16
VMEM = pl.BlockSpec(memory_space=pltpu.VMEM)
SMEM = pl.BlockSpec(memory_space=pltpu.SMEM)


def params():
    return pltpu.CompilerParams(vmem_limit_bytes=32 * 1024 * 1024)


def code_tiles(bases, waves, scales, first_blocks, store):
    coded = []
    for base, wave, scale in zip(bases, waves, scales):
        product = lax.dot_general(
            base, wave, (((0,), (0,)), ((), ())), preferred_element_type=jnp.float32
        )
        n = product.shape[1] // 2
        blocks = []
        for k in range(product.shape[0] // (2 * RB)):
            top = product[2 * RB * k : 2 * RB * k + RB]
            low = product[2 * RB * k + RB : 2 * RB * (k + 1)]
            both = jnp.concatenate([top[:, :n] + low[:, n:], top[:, n:] - low[:, :n]], 0)
            blocks.append((both * scale).astype(jnp.bfloat16))
        coded.append(blocks)
    for k, block in enumerate(coded[0]):
        store(min(k, CAP - 1), block)
    for k in reversed(range(len(coded[1]))):
        store(jnp.minimum(first_blocks + k, CAP - 1), coded[1][k])


def open_slots(load, counts, tile, blocks):
    rows = []
    for k in range(blocks):
        slot = min(k, CAP - 1) if tile == 0 else jnp.minimum(counts[0] + k, CAP - 1)
        block = load(slot)
        block = jnp.where(k < counts[tile], block, jnp.zeros_like(block))
        real, imag = block[:RB], block[RB:]
        rows.append(jnp.concatenate([real, imag], 1))
        rows.append(jnp.concatenate([-imag, real], 1))
    return jnp.concatenate(rows, 0)


def counts_of(ranks_ref, group, column):
    return ranks_ref[2 * group, column] // RB, ranks_ref[2 * group + 1, column] // RB


def far_first(tiles):
    bits = tiles.bit_length() - 1
    low, high = 2 ** (bits // 2), 2 ** (bits - bits // 2)
    return high, low, low, 1


def near_first(tiles):
    count_a, s1, count_b, s2 = far_first(tiles)
    return count_b, s2, count_a, s1


def at_once(tiles):
    return None


def exchange(blocks, route, tiles):
    if route is None:
        return [lax.all_to_all(blocks[0], "tile", split_axis=0, concat_axis=0, tiled=True)], []
    count_a, s1, count_b, s2 = route

    def swap(block, offset):
        return lax.ppermute(block, "tile", [(i, i ^ offset) for i in range(tiles)])

    hops = {a: swap(blocks[a], a * s1) for a in range(1, count_a)}
    first = [blocks[0]] + [hops[a] for a in range(1, count_a)]
    sends = [jnp.stack([first[a][b] for a in range(count_a)]) for b in range(1, count_b)]
    return first, sends


def second_hop(first, sends, route, tiles):
    if route is None:
        return first
    count_a, s1, count_b, s2 = route

    def swap(block, offset):
        return lax.ppermute(block, "tile", [(i, i ^ offset) for i in range(tiles)])

    hops = {b: swap(sends[b - 1], b * s2) for b in range(1, count_b)}
    return first + [hops[b] for b in range(1, count_b)]


def after(values, others):
    return lax.optimization_barrier((list(values), list(others)))[0]


def shapes_sent(route, tiles, shape):
    if route is None:
        return [jax.ShapeDtypeStruct((tiles,) + shape, jnp.bfloat16)]
    return [jax.ShapeDtypeStruct((route[2],) + shape, jnp.bfloat16)] * route[0]


def n_arrays(route):
    return 1 if route is None else route[0] + route[2] - 1


def each_arrival(route, me, refs, visit):
    if route is None:

        def direct(i, carry):
            visit(i, lambda slot: refs[0][i, slot])
            return carry

        lax.fori_loop(0, refs[0].shape[0], direct, 0, unroll=4)
        return
    count_a, s1, count_b, s2 = route
    for a in range(count_a):
        visit(me ^ (a * s1), lambda slot, a=a: refs[a][0, slot])
    for b in range(1, count_b):
        ref = refs[count_a + b - 1]

        def step(a, carry, ref=ref, b=b):
            visit(me ^ (a * s1) ^ (b * s2), lambda slot: ref[a, slot])
            return carry

        lax.fori_loop(0, count_a, step, 0, unroll=4)


def each_departure(route, me, refs, visit):
    for a, ref in enumerate(refs):

        def step(b, carry, ref=ref, a=a):
            def store(slot, block):
                ref[b, slot] = block

            visit(b if route is None else me ^ (a * route[1]) ^ (b * route[3]), store)
            return carry

        lax.fori_loop(0, ref.shape[0], step, 0, unroll=4)


def coded_kernel(route, me_ref, ranks_ref, scale_ref, v_ref, x_ref, *out_refs):
    me = me_ref[0]

    def visit(group, store):
        first, _ = counts_of(ranks_ref, group, me)
        wave = x_ref[...]
        code_tiles(
            [v_ref[2 * group], v_ref[2 * group + 1]],
            [wave, wave],
            [scale_ref[2 * group, me], scale_ref[2 * group + 1, me]],
            first,
            store,
        )

    each_departure(route, me, out_refs, visit)


def middle_kernel(route_in, route_out, tiles, *refs):
    me_ref, ranks_ref, scale_ref, u_ref = refs[:4]
    in_refs, y_ref, out_refs, rhs = (
        refs[4 : 4 + n_arrays(route_in)],
        refs[4 + n_arrays(route_in)],
        refs[5 + n_arrays(route_in) : -1],
        refs[-1],
    )
    me = me_ref[0]
    blocks = u_ref.shape[3] // (2 * RB)

    def unpack(column, load):
        counts = counts_of(ranks_ref, me, column)
        for tile in range(2):
            rhs[tile, column] = open_slots(load, counts, tile, blocks)

    each_arrival(route_in, me, in_refs, unpack)
    for tile in range(2):

        def add(pair, total):
            left = jnp.concatenate([u_ref[tile, 2 * pair], u_ref[tile, 2 * pair + 1]], 1)
            right = jnp.concatenate([rhs[tile, 2 * pair], rhs[tile, 2 * pair + 1]], 0)
            return total + jnp.dot(left, right, preferred_element_type=jnp.float32)

        total = jnp.zeros(y_ref.shape[1:], jnp.float32)
        y_ref[tile] = lax.fori_loop(0, tiles // 2, add, total, unroll=8).astype(jnp.bfloat16)

    def visit(column, store):
        first, _ = counts_of(ranks_ref, me, column)
        code_tiles(
            [u_ref[0, column], u_ref[1, column]],
            [y_ref[0], y_ref[1]],
            [scale_ref[2 * me, column], scale_ref[2 * me + 1, column]],
            first,
            store,
        )

    each_departure(route_out, me, out_refs, visit)


def adjoint_kernel(route, tiles, *refs):
    me_ref, ranks_ref, v_ref, in_refs, z_ref, rhs = *refs[:3], refs[3:-2], *refs[-2:]
    me = me_ref[0]
    blocks = v_ref.shape[2] // (2 * RB)

    def unpack(group, load):
        counts = counts_of(ranks_ref, group, me)
        rhs[group] = jnp.concatenate([open_slots(load, counts, t, blocks) for t in range(2)], 0)

    each_arrival(route, me, in_refs, unpack)

    def add(group, total):
        left = jnp.concatenate([v_ref[2 * group], v_ref[2 * group + 1]], 1)
        return total + jnp.dot(left, rhs[group], preferred_element_type=jnp.float32)

    total = lax.fori_loop(0, tiles, add, jnp.zeros(z_ref.shape, jnp.float32), unroll=8)
    z_ref[...] = total.astype(jnp.bfloat16)


def order_rows_kernel(core_ref, first_ref, second_ref, out_ref):
    n = first_ref.shape[1] // 2
    swapped = core_ref[0] == 1
    first, second = first_ref[...], second_ref[...]
    low = jnp.where(swapped, second, first)
    high = jnp.where(swapped, first, second)
    out_ref[:, 0 * n : 1 * n] = low[:, :n]
    out_ref[:, 1 * n : 2 * n] = high[:, :n]
    out_ref[:, 2 * n : 3 * n] = low[:, n:]
    out_ref[:, 3 * n : 4 * n] = high[:, n:]


def order_parts_kernel(core_ref, first_ref, second_ref, out_ref):
    out_ref[core_ref[0]] = first_ref[...]
    out_ref[1 - core_ref[0]] = second_ref[...]


WAYS = {"1a": far_first, "1b": near_first, "2a": far_first, "2b": at_once}


def per_device(wave_in, column_basis, row_basis, tile_scale, tile_ranks):
    tiles = lax.axis_size("tile")
    core = lax.axis_index("freq").astype(jnp.int32)
    core_at = core.reshape(1)
    me = lax.axis_index("tile").astype(jnp.int32).reshape(1)
    v = column_basis.reshape(column_basis.shape[1], *column_basis.shape[3:])
    u = row_basis[0]
    scales, ranks = tile_scale[0], tile_ranks[0]
    height, width = v.shape[1], v.shape[2]
    n = wave_in.shape[3]
    slots = (CAP, 2 * RB, n)
    swap = [(0, 1), (1, 0)]
    way = {name: pick(tiles) for name, pick in WAYS.items()}

    def cost(products, operands):
        return pl.CostEstimate(
            flops=4 * products * tiles * height * width * 2 * n,
            bytes_accessed=sum(a.size * a.dtype.itemsize for a in operands),
            transcendentals=0,
        )

    def code(x, route):
        shapes = shapes_sent(route, tiles, slots)
        return pl.pallas_call(
            lambda *refs: coded_kernel(route, *refs),
            out_shape=shapes,
            in_specs=[SMEM, SMEM, SMEM, VMEM, VMEM],
            out_specs=[VMEM] * len(shapes),
            compiler_params=params(),
            cost_estimate=cost(1, [v, x]),
        )(me, ranks, scales, v, x)

    def middle(arrived, route_in, route_out):
        shapes = shapes_sent(route_out, tiles, slots)
        result = pl.pallas_call(
            lambda *refs: middle_kernel(route_in, route_out, tiles, *refs),
            out_shape=[jax.ShapeDtypeStruct((2, height, 2 * n), jnp.bfloat16)] + shapes,
            in_specs=[SMEM, SMEM, SMEM, VMEM] + [VMEM] * len(arrived),
            out_specs=[VMEM] * (1 + len(shapes)),
            scratch_shapes=[pltpu.VMEM((2, tiles, width, 2 * n), jnp.bfloat16)],
            compiler_params=params(),
            cost_estimate=cost(2, [u, *arrived]),
        )(me, ranks, scales, u, *arrived)
        return result[0].reshape(2 * height, 2 * n), result[1:]

    def adjoint(arrived, route):
        return pl.pallas_call(
            lambda *refs: adjoint_kernel(route, tiles, *refs),
            out_shape=jax.ShapeDtypeStruct((height, 2 * n), jnp.bfloat16),
            in_specs=[SMEM, SMEM, VMEM] + [VMEM] * len(arrived),
            out_specs=VMEM,
            scratch_shapes=[pltpu.VMEM((tiles, 2 * width, 2 * n), jnp.bfloat16)],
            compiler_params=params(),
            cost_estimate=cost(1, [v, *arrived]),
        )(me, ranks, v, *arrived)

    def ordered(kernel, first, second, shape):
        return pl.pallas_call(
            kernel,
            out_shape=jax.ShapeDtypeStruct(shape, jnp.bfloat16),
            in_specs=[SMEM, VMEM, VMEM],
            out_specs=VMEM,
            compiler_params=params(),
        )(core_at, first, second)

    theirs = lax.dynamic_index_in_dim(wave_in, 1 - core, 0, keepdims=False)
    mine = lax.dynamic_index_in_dim(wave_in, core, 0, keepdims=False)
    other = lax.ppermute(theirs, "freq", swap)
    first_a, sends_a = exchange(code(mine.reshape(height, 2 * n), way["1a"]), way["1a"], tiles)
    first_b, sends_b = exchange(code(other.reshape(height, 2 * n), way["1b"]), way["1b"], tiles)
    coded_a = second_hop(first_a, sends_a, way["1a"], tiles)
    coded_b = second_hop(first_b, sends_b, way["1b"], tiles)
    y_a, back_a = middle(coded_a, way["1a"], way["2a"])
    first_a, sends_a = exchange(back_a, way["2a"], tiles)
    coded_b = after(coded_b, back_a)
    y_b, back_b = middle(coded_b, way["1b"], way["2b"])
    first_b, sends_b = exchange(back_b, way["2b"], tiles)
    back_a = second_hop(first_a, sends_a, way["2a"], tiles)
    back_b = second_hop(first_b, sends_b, way["2b"], tiles)
    z_a = adjoint(back_a, way["2a"])
    forward_out = ordered(order_rows_kernel, y_a, y_b, (2 * height, 4 * n))
    forward_out = forward_out.reshape(1, 2 * height, 2, 2 * n)
    z_b = lax.ppermute(adjoint(back_b, way["2b"]), "freq", swap)
    adjoint_out = ordered(order_parts_kernel, z_a, z_b, (2, height, 2 * n))
    return forward_out, adjoint_out.reshape(2, height, 2, n)


def solution(mesh):
    return jax.shard_map(
        per_device,
        mesh=mesh,
        in_specs=(
            P(None, "tile", None, "freq"),
            P("freq", None, "tile", None, None),
            P("freq", "tile", None, None, None),
            P("freq", None, None),
            P("freq", None, None),
        ),
        out_specs=(P("freq", "tile", None, None), P(None, "tile", None, "freq")),
        check_vma=False,
    )
```

```python
import jax
import jax.numpy as jnp
from jax import lax
from jax.experimental import pallas as pl
from jax.experimental.pallas import tpu as pltpu
from jax.sharding import PartitionSpec as P

CAP = 5
RB = 16
VMEM = pl.BlockSpec(memory_space=pltpu.VMEM)
SMEM = pl.BlockSpec(memory_space=pltpu.SMEM)


def params():
    return pltpu.CompilerParams(vmem_limit_bytes=32 * 1024 * 1024)


def code_tiles(bases, waves, scales, first_blocks, store):
    coded = []
    for base, wave, scale in zip(bases, waves, scales):
        product = lax.dot_general(
            base, wave, (((0,), (0,)), ((), ())), preferred_element_type=jnp.float32
        )
        n = product.shape[1] // 2
        blocks = []
        for k in range(product.shape[0] // (2 * RB)):
            top = product[2 * RB * k : 2 * RB * k + RB]
            low = product[2 * RB * k + RB : 2 * RB * (k + 1)]
            both = jnp.concatenate([top[:, :n] + low[:, n:], top[:, n:] - low[:, :n]], 0)
            blocks.append((both * scale).astype(jnp.bfloat16))
        coded.append(blocks)
    for k, block in enumerate(coded[0]):
        store(min(k, CAP - 1), block)
    for k in reversed(range(len(coded[1]))):
        store(jnp.minimum(first_blocks + k, CAP - 1), coded[1][k])


def open_slots(load, counts, tile, blocks):
    rows = []
    for k in range(blocks):
        slot = min(k, CAP - 1) if tile == 0 else jnp.minimum(counts[0] + k, CAP - 1)
        block = load(slot)
        block = jnp.where(k < counts[tile], block, jnp.zeros_like(block))
        real, imag = block[:RB], block[RB:]
        rows.append(jnp.concatenate([real, imag], 1))
        rows.append(jnp.concatenate([-imag, real], 1))
    return jnp.concatenate(rows, 0)


def counts_of(ranks_ref, group, column):
    return ranks_ref[column, 2 * group] // RB, ranks_ref[column, 2 * group + 1] // RB


def far_first(tiles):
    bits = tiles.bit_length() - 1
    low, high = 2 ** (bits // 2), 2 ** (bits - bits // 2)
    return high, low, low, 1


def near_first(tiles):
    count_a, s1, count_b, s2 = far_first(tiles)
    return count_b, s2, count_a, s1


def at_once(tiles):
    return None


def exchange(blocks, route, tiles):
    if route is None:
        return [lax.all_to_all(blocks[0], "tile", split_axis=0, concat_axis=0, tiled=True)], []
    count_a, s1, count_b, s2 = route

    def swap(block, offset):
        return lax.ppermute(block, "tile", [(i, i ^ offset) for i in range(tiles)])

    hops = {a: swap(blocks[a], a * s1) for a in range(1, count_a)}
    first = [blocks[0]] + [hops[a] for a in range(1, count_a)]
    sends = [jnp.stack([first[a][b] for a in range(count_a)]) for b in range(1, count_b)]
    return first, sends


def second_hop(first, sends, route, tiles):
    if route is None:
        return first
    count_a, s1, count_b, s2 = route

    def swap(block, offset):
        return lax.ppermute(block, "tile", [(i, i ^ offset) for i in range(tiles)])

    hops = {b: swap(sends[b - 1], b * s2) for b in range(1, count_b)}
    return first + [hops[b] for b in reversed(range(1, count_b))]


def after(values, others):
    return lax.optimization_barrier((list(values), list(others)))[0]


def shapes_sent(route, tiles, shape):
    if route is None:
        return [jax.ShapeDtypeStruct((tiles,) + shape, jnp.bfloat16)]
    return [jax.ShapeDtypeStruct((route[2],) + shape, jnp.bfloat16)] * route[0]


def n_arrays(route):
    return 1 if route is None else route[0] + route[2] - 1


def each_arrival(route, me, refs, visit):
    if route is None:

        def direct(i, carry):
            visit(i, lambda slot: refs[0][i, slot])
            return carry

        lax.fori_loop(0, refs[0].shape[0], direct, 0, unroll=4)
        return
    count_a, s1, count_b, s2 = route
    for a in range(count_a):
        visit(me ^ (a * s1), lambda slot, a=a: refs[a][0, slot])
    for b in range(1, count_b):
        ref = refs[count_a + count_b - 1 - b]

        def step(a, carry, ref=ref, b=b):
            visit(me ^ (a * s1) ^ (b * s2), lambda slot: ref[a, slot])
            return carry

        lax.fori_loop(0, count_a, step, 0, unroll=4)


def each_departure(route, me, refs, visit):
    for a, ref in enumerate(refs):

        def step(b, carry, ref=ref, a=a):
            def store(slot, block):
                ref[b, slot] = block

            visit(b if route is None else me ^ (a * route[1]) ^ (b * route[3]), store)
            return carry

        lax.fori_loop(0, ref.shape[0], step, 0, unroll=4)


def coded_kernel(route, me_ref, ranks_ref, scale_ref, v_ref, x_ref, *out_refs):
    me = me_ref[0]

    def visit(group, store):
        first, _ = counts_of(ranks_ref, group, me)
        wave = x_ref[...]
        code_tiles(
            [v_ref[2 * group], v_ref[2 * group + 1]],
            [wave, wave],
            [scale_ref[me, 2 * group], scale_ref[me, 2 * group + 1]],
            first,
            store,
        )

    each_departure(route, me, out_refs, visit)


def middle_kernel(route_in, route_out, tiles, *refs):
    me_ref, ranks_ref, scale_ref, u_ref = refs[:4]
    in_refs, y_ref, out_refs, rhs = (
        refs[4 : 4 + n_arrays(route_in)],
        refs[4 + n_arrays(route_in)],
        refs[5 + n_arrays(route_in) : -1],
        refs[-1],
    )
    me = me_ref[0]
    blocks = u_ref.shape[3] // (2 * RB)

    def unpack(column, load):
        counts = counts_of(ranks_ref, me, column)
        for tile in range(2):
            rhs[tile, column] = open_slots(load, counts, tile, blocks)

    each_arrival(route_in, me, in_refs, unpack)
    for tile in range(2):

        def add(pair, total):
            left = jnp.concatenate([u_ref[tile, 2 * pair], u_ref[tile, 2 * pair + 1]], 1)
            right = jnp.concatenate([rhs[tile, 2 * pair], rhs[tile, 2 * pair + 1]], 0)
            return total + jnp.dot(left, right, preferred_element_type=jnp.float32)

        total = jnp.zeros(y_ref.shape[1:], jnp.float32)
        y_ref[tile] = lax.fori_loop(0, tiles // 2, add, total, unroll=8).astype(jnp.bfloat16)

    def visit(column, store):
        first, _ = counts_of(ranks_ref, me, column)
        code_tiles(
            [u_ref[0, column], u_ref[1, column]],
            [y_ref[0], y_ref[1]],
            [scale_ref[column, 2 * me], scale_ref[column, 2 * me + 1]],
            first,
            store,
        )

    each_departure(route_out, me, out_refs, visit)


def adjoint_kernel(route, tiles, *refs):
    me_ref, ranks_ref, v_ref, in_refs, z_ref, rhs = *refs[:3], refs[3:-2], *refs[-2:]
    me = me_ref[0]
    blocks = v_ref.shape[2] // (2 * RB)

    def unpack(group, load):
        counts = counts_of(ranks_ref, group, me)
        rhs[group] = jnp.concatenate([open_slots(load, counts, t, blocks) for t in range(2)], 0)

    each_arrival(route, me, in_refs, unpack)

    def add(group, total):
        left = jnp.concatenate([v_ref[2 * group], v_ref[2 * group + 1]], 1)
        return total + jnp.dot(left, rhs[group], preferred_element_type=jnp.float32)

    total = lax.fori_loop(0, tiles, add, jnp.zeros(z_ref.shape, jnp.float32), unroll=8)
    z_ref[...] = total.astype(jnp.bfloat16)


def order_rows_kernel(core_ref, first_ref, second_ref, out_ref):
    n = first_ref.shape[1] // 2
    swapped = core_ref[0] == 1
    first, second = first_ref[...], second_ref[...]
    low = jnp.where(swapped, second, first)
    high = jnp.where(swapped, first, second)
    out_ref[:, 0 * n : 1 * n] = low[:, :n]
    out_ref[:, 1 * n : 2 * n] = high[:, :n]
    out_ref[:, 2 * n : 3 * n] = low[:, n:]
    out_ref[:, 3 * n : 4 * n] = high[:, n:]


def order_parts_kernel(core_ref, first_ref, second_ref, out_ref):
    out_ref[core_ref[0]] = first_ref[...]
    out_ref[1 - core_ref[0]] = second_ref[...]


WAYS = {"1a": far_first, "1b": near_first, "2a": far_first, "2b": at_once}


def per_device(wave_in, column_basis, row_basis, tile_scale, tile_ranks):
    tiles = lax.axis_size("tile")
    core = lax.axis_index("freq").astype(jnp.int32)
    core_at = core.reshape(1)
    me = lax.axis_index("tile").astype(jnp.int32).reshape(1)
    v = column_basis.reshape(column_basis.shape[1], *column_basis.shape[3:])
    u = row_basis[0]
    scales, ranks = tile_scale[0].T, tile_ranks[0].T
    height, width = v.shape[1], v.shape[2]
    n = wave_in.shape[3]
    slots = (CAP, 2 * RB, n)
    swap = [(0, 1), (1, 0)]
    way = {name: pick(tiles) for name, pick in WAYS.items()}

    def cost(products, operands, weight=1):
        return pl.CostEstimate(
            flops=weight * 4 * products * tiles * height * width * 2 * n,
            bytes_accessed=weight * sum(a.size * a.dtype.itemsize for a in operands),
            transcendentals=0,
        )

    def code(x, route):
        shapes = shapes_sent(route, tiles, slots)
        return pl.pallas_call(
            lambda *refs: coded_kernel(route, *refs),
            out_shape=shapes,
            in_specs=[SMEM, SMEM, SMEM, VMEM, VMEM],
            out_specs=[VMEM] * len(shapes),
            compiler_params=params(),
            cost_estimate=cost(1, [v, x]),
        )(me, ranks, scales, v, x)

    def middle(arrived, route_in, route_out):
        shapes = shapes_sent(route_out, tiles, slots)
        result = pl.pallas_call(
            lambda *refs: middle_kernel(route_in, route_out, tiles, *refs),
            out_shape=[jax.ShapeDtypeStruct((2, height, 2 * n), jnp.bfloat16)] + shapes,
            in_specs=[SMEM, SMEM, SMEM, VMEM] + [VMEM] * len(arrived),
            out_specs=[VMEM] * (1 + len(shapes)),
            scratch_shapes=[pltpu.VMEM((2, tiles, width, 2 * n), jnp.bfloat16)],
            compiler_params=params(),
            cost_estimate=cost(2, [u, *arrived], 10),
        )(me, ranks, scales, u, *arrived)
        return result[0].reshape(2 * height, 2 * n), result[1:]

    def adjoint(arrived, route):
        return pl.pallas_call(
            lambda *refs: adjoint_kernel(route, tiles, *refs),
            out_shape=jax.ShapeDtypeStruct((height, 2 * n), jnp.bfloat16),
            in_specs=[SMEM, SMEM, VMEM] + [VMEM] * len(arrived),
            out_specs=VMEM,
            scratch_shapes=[pltpu.VMEM((tiles, 2 * width, 2 * n), jnp.bfloat16)],
            compiler_params=params(),
            cost_estimate=cost(1, [v, *arrived]),
        )(me, ranks, v, *arrived)

    def ordered(kernel, first, second, shape):
        return pl.pallas_call(
            kernel,
            out_shape=jax.ShapeDtypeStruct(shape, jnp.bfloat16),
            in_specs=[SMEM, VMEM, VMEM],
            out_specs=VMEM,
            compiler_params=params(),
        )(core_at, first, second)

    theirs = lax.dynamic_index_in_dim(wave_in, 1 - core, 0, keepdims=False)
    mine = lax.dynamic_index_in_dim(wave_in, core, 0, keepdims=False)
    other = lax.ppermute(theirs, "freq", swap)
    coded_a = code(other.reshape(height, 2 * n), way["1a"])
    first_a, sends_a = exchange(coded_a, way["1a"], tiles)
    (mine,) = after([mine], coded_a)
    first_b, sends_b = exchange(code(mine.reshape(height, 2 * n), way["1b"]), way["1b"], tiles)
    coded_a = second_hop(first_a, sends_a, way["1a"], tiles)
    coded_b = second_hop(first_b, sends_b, way["1b"], tiles)
    y_a, back_a = middle(coded_a, way["1a"], way["2a"])
    first_a, sends_a = exchange(back_a, way["2a"], tiles)
    coded_b = after(coded_b, back_a)
    y_b, back_b = middle(coded_b, way["1b"], way["2b"])
    first_b, sends_b = exchange(back_b, way["2b"], tiles)
    back_a = second_hop(first_a, sends_a, way["2a"], tiles)
    back_b = second_hop(first_b, sends_b, way["2b"], tiles)
    z_a = lax.ppermute(adjoint(back_a, way["2a"]), "freq", swap)
    forward_out = ordered(order_rows_kernel, y_b, y_a, (2 * height, 4 * n))
    forward_out = forward_out.reshape(1, 2 * height, 2, 2 * n)
    z_b = adjoint(back_b, way["2b"])
    adjoint_out = ordered(order_parts_kernel, z_b, z_a, (2, height, 2 * n))
    return forward_out, adjoint_out.reshape(2, height, 2, n)


def solution(mesh):
    return jax.shard_map(
        per_device,
        mesh=mesh,
        in_specs=(
            P(None, "tile", None, "freq"),
            P("freq", None, "tile", None, None),
            P("freq", "tile", None, None, None),
            P("freq", None, None),
            P("freq", None, None),
        ),
        out_specs=(P("freq", "tile", None, None), P(None, "tile", None, "freq")),
        check_vma=False,
    )
```

```python
import jax
import jax.numpy as jnp
from jax import lax
from jax.experimental import pallas as pl
from jax.experimental.pallas import tpu as pltpu
from jax.sharding import PartitionSpec as P

CAP = 5
RB = 16
VMEM = pl.BlockSpec(memory_space=pltpu.VMEM)
SMEM = pl.BlockSpec(memory_space=pltpu.SMEM)


def params():
    return pltpu.CompilerParams(vmem_limit_bytes=32 * 1024 * 1024)


def code_tiles(bases, waves, scales, first_blocks, store):
    coded = []
    for base, wave, scale in zip(bases, waves, scales):
        product = lax.dot_general(
            base, wave, (((0,), (0,)), ((), ())), preferred_element_type=jnp.float32
        )
        n = product.shape[1] // 2
        blocks = []
        for k in range(product.shape[0] // (2 * RB)):
            top = product[2 * RB * k : 2 * RB * k + RB]
            low = product[2 * RB * k + RB : 2 * RB * (k + 1)]
            both = jnp.concatenate([top[:, :n] + low[:, n:], top[:, n:] - low[:, :n]], 0)
            blocks.append((both * scale).astype(jnp.bfloat16))
        coded.append(blocks)
    for k, block in enumerate(coded[0]):
        store(min(k, CAP - 1), block)
    for k in reversed(range(len(coded[1]))):
        store(jnp.minimum(first_blocks + k, CAP - 1), coded[1][k])


def open_slots(load, counts, tile, blocks):
    rows = []
    for k in range(blocks):
        slot = min(k, CAP - 1) if tile == 0 else jnp.minimum(counts[0] + k, CAP - 1)
        block = load(slot)
        block = jnp.where(k < counts[tile], block, jnp.zeros_like(block))
        real, imag = block[:RB], block[RB:]
        rows.append(jnp.concatenate([real, imag], 1))
        rows.append(jnp.concatenate([-imag, real], 1))
    return jnp.concatenate(rows, 0)


def counts_of(ranks_ref, group, column):
    return ranks_ref[column, 2 * group] // RB, ranks_ref[column, 2 * group + 1] // RB


def far_first(tiles):
    bits = tiles.bit_length() - 1
    low, high = 2 ** (bits // 2), 2 ** (bits - bits // 2)
    return high, low, low, 1


def near_first(tiles):
    count_a, s1, count_b, s2 = far_first(tiles)
    return count_b, s2, count_a, s1


def at_once(tiles):
    return None


def exchange(blocks, route, tiles):
    if route is None:
        return [lax.all_to_all(blocks[0], "tile", split_axis=0, concat_axis=0, tiled=True)], []
    count_a, s1, count_b, s2 = route

    def swap(block, offset):
        return lax.ppermute(block, "tile", [(i, i ^ offset) for i in range(tiles)])

    hops = {a: swap(blocks[a], a * s1) for a in range(1, count_a)}
    first = [blocks[0]] + [hops[a] for a in range(1, count_a)]
    sends = [jnp.stack([first[a][b] for a in range(count_a)]) for b in range(1, count_b)]
    return first, sends


def second_hop(first, sends, route, tiles):
    if route is None:
        return first
    count_a, s1, count_b, s2 = route

    def swap(block, offset):
        return lax.ppermute(block, "tile", [(i, i ^ offset) for i in range(tiles)])

    hops = {b: swap(sends[b - 1], b * s2) for b in range(1, count_b)}
    return first + [hops[b] for b in reversed(range(1, count_b))]


def after(values, others):
    return lax.optimization_barrier((list(values), list(others)))[0]


def shapes_sent(route, tiles, shape):
    if route is None:
        return [jax.ShapeDtypeStruct((tiles,) + shape, jnp.bfloat16)]
    return [jax.ShapeDtypeStruct((route[2],) + shape, jnp.bfloat16)] * route[0]


def n_arrays(route):
    return 1 if route is None else route[0] + route[2] - 1


def each_arrival(route, me, refs, visit):
    if route is None:

        def direct(i, carry):
            visit(i, lambda slot: refs[0][i, slot])
            return carry

        lax.fori_loop(0, refs[0].shape[0], direct, 0, unroll=4)
        return
    count_a, s1, count_b, s2 = route
    for a in range(count_a):
        visit(me ^ (a * s1), lambda slot, a=a: refs[a][0, slot])
    for b in range(1, count_b):
        ref = refs[count_a + count_b - 1 - b]

        def step(a, carry, ref=ref, b=b):
            visit(me ^ (a * s1) ^ (b * s2), lambda slot: ref[a, slot])
            return carry

        lax.fori_loop(0, count_a, step, 0, unroll=4)


def each_departure(route, me, refs, visit):
    for a, ref in enumerate(refs):

        def step(b, carry, ref=ref, a=a):
            def store(slot, block):
                ref[b, slot] = block

            visit(b if route is None else me ^ (a * route[1]) ^ (b * route[3]), store)
            return carry

        lax.fori_loop(0, ref.shape[0], step, 0, unroll=4)


def coded_kernel(route, me_ref, ranks_ref, scale_ref, v_ref, x_ref, *out_refs):
    me = me_ref[0]

    def visit(group, store):
        first, _ = counts_of(ranks_ref, group, me)
        wave = x_ref[...]
        code_tiles(
            [v_ref[2 * group], v_ref[2 * group + 1]],
            [wave, wave],
            [scale_ref[me, 2 * group], scale_ref[me, 2 * group + 1]],
            first,
            store,
        )

    each_departure(route, me, out_refs, visit)


def middle_kernel(route_in, route_out, tiles, *refs):
    me_ref, ranks_ref, scale_ref, u_ref = refs[:4]
    in_refs, y_ref, out_refs, rhs = (
        refs[4 : 4 + n_arrays(route_in)],
        refs[4 + n_arrays(route_in)],
        refs[5 + n_arrays(route_in) : -1],
        refs[-1],
    )
    me = me_ref[0]
    blocks = u_ref.shape[3] // (2 * RB)

    def unpack(column, load):
        counts = counts_of(ranks_ref, me, column)
        for tile in range(2):
            rhs[tile, column] = open_slots(load, counts, tile, blocks)

    each_arrival(route_in, me, in_refs, unpack)
    for tile in range(2):

        def add(pair, total):
            left = jnp.concatenate([u_ref[tile, 2 * pair], u_ref[tile, 2 * pair + 1]], 1)
            right = jnp.concatenate([rhs[tile, 2 * pair], rhs[tile, 2 * pair + 1]], 0)
            return total + jnp.dot(left, right, preferred_element_type=jnp.float32)

        total = jnp.zeros(y_ref.shape[1:], jnp.float32)
        y_ref[tile] = lax.fori_loop(0, tiles // 2, add, total, unroll=8).astype(jnp.bfloat16)

    def visit(column, store):
        first, _ = counts_of(ranks_ref, me, column)
        code_tiles(
            [u_ref[0, column], u_ref[1, column]],
            [y_ref[0], y_ref[1]],
            [scale_ref[column, 2 * me], scale_ref[column, 2 * me + 1]],
            first,
            store,
        )

    each_departure(route_out, me, out_refs, visit)


def adjoint_kernel(route, tiles, *refs):
    me_ref, ranks_ref, v_ref, in_refs, z_ref, rhs = *refs[:3], refs[3:-2], *refs[-2:]
    me = me_ref[0]
    blocks = v_ref.shape[2] // (2 * RB)

    def unpack(group, load):
        counts = counts_of(ranks_ref, group, me)
        rhs[group] = jnp.concatenate([open_slots(load, counts, t, blocks) for t in range(2)], 0)

    each_arrival(route, me, in_refs, unpack)

    def add(group, total):
        left = jnp.concatenate([v_ref[2 * group], v_ref[2 * group + 1]], 1)
        return total + jnp.dot(left, rhs[group], preferred_element_type=jnp.float32)

    total = lax.fori_loop(0, tiles, add, jnp.zeros(z_ref.shape, jnp.float32), unroll=8)
    z_ref[...] = total.astype(jnp.bfloat16)


def order_rows_kernel(core_ref, first_ref, second_ref, out_ref):
    n = first_ref.shape[1] // 2
    swapped = core_ref[0] == 1
    first, second = first_ref[...], second_ref[...]
    low = jnp.where(swapped, second, first)
    high = jnp.where(swapped, first, second)
    out_ref[:, 0 * n : 1 * n] = low[:, :n]
    out_ref[:, 1 * n : 2 * n] = high[:, :n]
    out_ref[:, 2 * n : 3 * n] = low[:, n:]
    out_ref[:, 3 * n : 4 * n] = high[:, n:]


def order_parts_kernel(core_ref, first_ref, second_ref, out_ref):
    out_ref[core_ref[0]] = first_ref[...]
    out_ref[1 - core_ref[0]] = second_ref[...]


WAYS = {"1a": far_first, "1b": near_first, "2a": far_first, "2b": at_once}


def per_device(wave_in, column_basis, row_basis, tile_scale, tile_ranks):
    tiles = lax.axis_size("tile")
    core = lax.axis_index("freq").astype(jnp.int32)
    core_at = core.reshape(1)
    me = lax.axis_index("tile").astype(jnp.int32).reshape(1)
    v = column_basis.reshape(column_basis.shape[1], *column_basis.shape[3:])
    u = row_basis[0]
    scales, ranks = tile_scale[0].T, tile_ranks[0].T
    height, width = v.shape[1], v.shape[2]
    n = wave_in.shape[3]
    slots = (CAP, 2 * RB, n)
    swap = [(0, 1), (1, 0)]
    way = {name: pick(tiles) for name, pick in WAYS.items()}

    def cost(products, operands, weight=1):
        return pl.CostEstimate(
            flops=weight * 4 * products * tiles * height * width * 2 * n,
            bytes_accessed=weight * sum(a.size * a.dtype.itemsize for a in operands),
            transcendentals=0,
        )

    def code(x, route):
        shapes = shapes_sent(route, tiles, slots)
        return pl.pallas_call(
            lambda *refs: coded_kernel(route, *refs),
            out_shape=shapes,
            in_specs=[SMEM, SMEM, SMEM, VMEM, VMEM],
            out_specs=[VMEM] * len(shapes),
            compiler_params=params(),
            cost_estimate=cost(1, [v, x]),
        )(me, ranks, scales, v, x)

    def middle(arrived, route_in, route_out):
        shapes = shapes_sent(route_out, tiles, slots)
        result = pl.pallas_call(
            lambda *refs: middle_kernel(route_in, route_out, tiles, *refs),
            out_shape=[jax.ShapeDtypeStruct((2, height, 2 * n), jnp.bfloat16)] + shapes,
            in_specs=[SMEM, SMEM, SMEM, VMEM] + [VMEM] * len(arrived),
            out_specs=[VMEM] * (1 + len(shapes)),
            scratch_shapes=[pltpu.VMEM((2, tiles, width, 2 * n), jnp.bfloat16)],
            compiler_params=params(),
            cost_estimate=cost(2, [u, *arrived], 10),
        )(me, ranks, scales, u, *arrived)
        return result[0].reshape(2 * height, 2 * n), result[1:]

    def adjoint(arrived, route):
        return pl.pallas_call(
            lambda *refs: adjoint_kernel(route, tiles, *refs),
            out_shape=jax.ShapeDtypeStruct((height, 2 * n), jnp.bfloat16),
            in_specs=[SMEM, SMEM, VMEM] + [VMEM] * len(arrived),
            out_specs=VMEM,
            scratch_shapes=[pltpu.VMEM((tiles, 2 * width, 2 * n), jnp.bfloat16)],
            compiler_params=params(),
            cost_estimate=cost(1, [v, *arrived]),
        )(me, ranks, v, *arrived)

    def ordered(kernel, first, second, shape):
        return pl.pallas_call(
            kernel,
            out_shape=jax.ShapeDtypeStruct(shape, jnp.bfloat16),
            in_specs=[SMEM, VMEM, VMEM],
            out_specs=VMEM,
            compiler_params=params(),
        )(core_at, first, second)

    theirs = lax.dynamic_index_in_dim(wave_in, 1 - core, 0, keepdims=False)
    mine = lax.dynamic_index_in_dim(wave_in, core, 0, keepdims=False)
    other = lax.ppermute(theirs, "freq", swap)
    coded_a = code(other.reshape(height, 2 * n), way["1a"])
    first_a, sends_a = exchange(coded_a, way["1a"], tiles)
    (mine,) = after([mine], coded_a)
    first_b, sends_b = exchange(code(mine.reshape(height, 2 * n), way["1b"]), way["1b"], tiles)
    coded_a = second_hop(first_a, sends_a, way["1a"], tiles)
    coded_b = second_hop(first_b, sends_b, way["1b"], tiles)
    y_a, back_a = middle(coded_a, way["1a"], way["2a"])
    farthest_b = coded_b[way["1b"][0]]
    back_a = [*back_a[:2], *after(back_a[2:], [farthest_b])]
    first_a, sends_a = exchange(back_a, way["2a"], tiles)
    coded_b = after(coded_b, back_a)
    y_b, back_b = middle(coded_b, way["1b"], way["2b"])
    first_b, sends_b = exchange(back_b, way["2b"], tiles)
    back_a = second_hop(first_a, sends_a, way["2a"], tiles)
    back_b = second_hop(first_b, sends_b, way["2b"], tiles)
    z_a = lax.ppermute(adjoint(back_a, way["2a"]), "freq", swap)
    forward_out = ordered(order_rows_kernel, y_b, y_a, (2 * height, 4 * n))
    forward_out = forward_out.reshape(1, 2 * height, 2, 2 * n)
    z_b = adjoint(back_b, way["2b"])
    adjoint_out = ordered(order_parts_kernel, z_b, z_a, (2, height, 2 * n))
    return forward_out, adjoint_out.reshape(2, height, 2, n)


def solution(mesh):
    return jax.shard_map(
        per_device,
        mesh=mesh,
        in_specs=(
            P(None, "tile", None, "freq"),
            P("freq", None, "tile", None, None),
            P("freq", "tile", None, None, None),
            P("freq", None, None),
            P("freq", None, None),
        ),
        out_specs=(P("freq", "tile", None, None), P(None, "tile", None, "freq")),
        check_vma=False,
    )
```

```python
import jax
import jax.numpy as jnp
from jax import lax
from jax.experimental import pallas as pl
from jax.experimental.pallas import tpu as pltpu
from jax.sharding import PartitionSpec as P

CAP = 5
RB = 16
VMEM = pl.BlockSpec(memory_space=pltpu.VMEM)
SMEM = pl.BlockSpec(memory_space=pltpu.SMEM)


def params():
    return pltpu.CompilerParams(vmem_limit_bytes=32 * 1024 * 1024)


def code_tiles(bases, waves, scales, first_blocks, store):
    coded = []
    for base, wave, scale in zip(bases, waves, scales):
        product = lax.dot_general(
            base, wave, (((0,), (0,)), ((), ())), preferred_element_type=jnp.float32
        )
        n = product.shape[1] // 2
        blocks = []
        for k in range(product.shape[0] // (2 * RB)):
            top = product[2 * RB * k : 2 * RB * k + RB]
            low = product[2 * RB * k + RB : 2 * RB * (k + 1)]
            both = jnp.concatenate([top[:, :n] + low[:, n:], top[:, n:] - low[:, :n]], 0)
            blocks.append((both * scale).astype(jnp.bfloat16))
        coded.append(blocks)
    for k, block in enumerate(coded[0]):
        store(min(k, CAP - 1), block)
    for k in reversed(range(len(coded[1]))):
        store(jnp.minimum(first_blocks + k, CAP - 1), coded[1][k])


def open_slots(load, counts, tile, blocks):
    rows = []
    for k in range(blocks):
        slot = min(k, CAP - 1) if tile == 0 else jnp.minimum(counts[0] + k, CAP - 1)
        block = load(slot)
        block = jnp.where(k < counts[tile], block, jnp.zeros_like(block))
        real, imag = block[:RB], block[RB:]
        rows.append(jnp.concatenate([real, imag], 1))
        rows.append(jnp.concatenate([-imag, real], 1))
    return jnp.concatenate(rows, 0)


def counts_of(ranks_ref, group, column):
    return ranks_ref[column, 2 * group] // RB, ranks_ref[column, 2 * group + 1] // RB


def far_first(tiles):
    bits = tiles.bit_length() - 1
    low, high = 2 ** (bits // 2), 2 ** (bits - bits // 2)
    return high, low, low, 1


def near_first(tiles):
    count_a, s1, count_b, s2 = far_first(tiles)
    return count_b, s2, count_a, s1


def at_once(tiles):
    return None


def exchange(blocks, route, tiles):
    if route is None:
        return [lax.all_to_all(blocks[0], "tile", split_axis=0, concat_axis=0, tiled=True)], []
    count_a, s1, count_b, s2 = route

    def swap(block, offset):
        return lax.ppermute(block, "tile", [(i, i ^ offset) for i in range(tiles)])

    hops = {a: swap(blocks[a], a * s1) for a in range(1, count_a)}
    first = [blocks[0]] + [hops[a] for a in range(1, count_a)]
    sends = [jnp.stack([first[a][b] for a in range(count_a)]) for b in range(1, count_b)]
    return first, sends


def second_hop(first, sends, route, tiles):
    if route is None:
        return first
    count_a, s1, count_b, s2 = route

    def swap(block, offset):
        return lax.ppermute(block, "tile", [(i, i ^ offset) for i in range(tiles)])

    hops = {b: swap(sends[b - 1], b * s2) for b in range(1, count_b)}
    return first + [hops[b] for b in reversed(range(1, count_b))]


def after(values, others):
    return lax.optimization_barrier((list(values), list(others)))[0]


def shapes_sent(route, tiles, shape):
    if route is None:
        return [jax.ShapeDtypeStruct((tiles,) + shape, jnp.bfloat16)]
    return [jax.ShapeDtypeStruct((route[2],) + shape, jnp.bfloat16)] * route[0]


def n_arrays(route):
    return 1 if route is None else route[0] + route[2] - 1


def each_arrival(route, me, refs, visit):
    if route is None:

        def direct(i, carry):
            visit(i, lambda slot: refs[0][i, slot])
            return carry

        lax.fori_loop(0, refs[0].shape[0], direct, 0, unroll=4)
        return
    count_a, s1, count_b, s2 = route
    for a in range(count_a):
        visit(me ^ (a * s1), lambda slot, a=a: refs[a][0, slot])
    for b in range(1, count_b):
        ref = refs[count_a + count_b - 1 - b]

        def step(a, carry, ref=ref, b=b):
            visit(me ^ (a * s1) ^ (b * s2), lambda slot: ref[a, slot])
            return carry

        lax.fori_loop(0, count_a, step, 0, unroll=4)


def each_departure(route, me, refs, visit):
    for a, ref in enumerate(refs):

        def step(b, carry, ref=ref, a=a):
            def store(slot, block):
                ref[b, slot] = block

            visit(b if route is None else me ^ (a * route[1]) ^ (b * route[3]), store)
            return carry

        lax.fori_loop(0, ref.shape[0], step, 0, unroll=4)


def coded_kernel(route, me_ref, ranks_ref, scale_ref, v_ref, x_ref, *out_refs):
    me = me_ref[0]

    def visit(group, store):
        first, _ = counts_of(ranks_ref, group, me)
        wave = x_ref[...]
        code_tiles(
            [v_ref[2 * group], v_ref[2 * group + 1]],
            [wave, wave],
            [scale_ref[me, 2 * group], scale_ref[me, 2 * group + 1]],
            first,
            store,
        )

    each_departure(route, me, out_refs, visit)


def middle_kernel(route_in, route_out, tiles, *refs):
    me_ref, ranks_ref, scale_ref, u_ref = refs[:4]
    in_refs, y_ref, out_refs, rhs = (
        refs[4 : 4 + n_arrays(route_in)],
        refs[4 + n_arrays(route_in)],
        refs[5 + n_arrays(route_in) : -1],
        refs[-1],
    )
    me = me_ref[0]
    blocks = u_ref.shape[3] // (2 * RB)

    def unpack(column, load):
        counts = counts_of(ranks_ref, me, column)
        for tile in range(2):
            rhs[tile, column] = open_slots(load, counts, tile, blocks)

    each_arrival(route_in, me, in_refs, unpack)
    for tile in range(2):

        def add(pair, total):
            left = jnp.concatenate([u_ref[tile, 2 * pair], u_ref[tile, 2 * pair + 1]], 1)
            right = jnp.concatenate([rhs[tile, 2 * pair], rhs[tile, 2 * pair + 1]], 0)
            return total + jnp.dot(left, right, preferred_element_type=jnp.float32)

        total = jnp.zeros(y_ref.shape[1:], jnp.float32)
        y_ref[tile] = lax.fori_loop(0, tiles // 2, add, total, unroll=8).astype(jnp.bfloat16)

    def visit(column, store):
        first, _ = counts_of(ranks_ref, me, column)
        code_tiles(
            [u_ref[0, column], u_ref[1, column]],
            [y_ref[0], y_ref[1]],
            [scale_ref[column, 2 * me], scale_ref[column, 2 * me + 1]],
            first,
            store,
        )

    each_departure(route_out, me, out_refs, visit)


def adjoint_kernel(route, tiles, *refs):
    me_ref, ranks_ref, v_ref, in_refs, z_ref, rhs = *refs[:3], refs[3:-2], *refs[-2:]
    me = me_ref[0]
    blocks = v_ref.shape[2] // (2 * RB)

    def unpack(group, load):
        counts = counts_of(ranks_ref, group, me)
        rhs[group] = jnp.concatenate([open_slots(load, counts, t, blocks) for t in range(2)], 0)

    each_arrival(route, me, in_refs, unpack)

    def add(group, total):
        left = jnp.concatenate([v_ref[2 * group], v_ref[2 * group + 1]], 1)
        return total + jnp.dot(left, rhs[group], preferred_element_type=jnp.float32)

    total = lax.fori_loop(0, tiles, add, jnp.zeros(z_ref.shape, jnp.float32), unroll=8)
    z_ref[...] = total.astype(jnp.bfloat16)


def order_rows_kernel(core_ref, first_ref, second_ref, out_ref):
    n = first_ref.shape[1] // 2
    swapped = core_ref[0] == 1
    first, second = first_ref[...], second_ref[...]
    low = jnp.where(swapped, second, first)
    high = jnp.where(swapped, first, second)
    out_ref[:, 0 * n : 1 * n] = low[:, :n]
    out_ref[:, 1 * n : 2 * n] = high[:, :n]
    out_ref[:, 2 * n : 3 * n] = low[:, n:]
    out_ref[:, 3 * n : 4 * n] = high[:, n:]


def order_parts_kernel(core_ref, first_ref, second_ref, out_ref):
    out_ref[core_ref[0]] = first_ref[...]
    out_ref[1 - core_ref[0]] = second_ref[...]


WAYS = {"1a": far_first, "1b": near_first, "2a": far_first, "2b": at_once}


def per_device(wave_in, column_basis, row_basis, tile_scale, tile_ranks):
    tiles = lax.axis_size("tile")
    core = lax.axis_index("freq").astype(jnp.int32)
    core_at = core.reshape(1)
    me = lax.axis_index("tile").astype(jnp.int32).reshape(1)
    v = column_basis.reshape(column_basis.shape[1], *column_basis.shape[3:])
    u = row_basis[0]
    scales, ranks = tile_scale[0].T, tile_ranks[0].T
    height, width = v.shape[1], v.shape[2]
    n = wave_in.shape[3]
    slots = (CAP, 2 * RB, n)
    swap = [(0, 1), (1, 0)]
    way = {name: pick(tiles) for name, pick in WAYS.items()}

    def cost(products, operands, weight=1):
        return pl.CostEstimate(
            flops=weight * 4 * products * tiles * height * width * 2 * n,
            bytes_accessed=weight * sum(a.size * a.dtype.itemsize for a in operands),
            transcendentals=0,
        )

    def code(x, route):
        shapes = shapes_sent(route, tiles, slots)
        return pl.pallas_call(
            lambda *refs: coded_kernel(route, *refs),
            out_shape=shapes,
            in_specs=[SMEM, SMEM, SMEM, VMEM, VMEM],
            out_specs=[VMEM] * len(shapes),
            compiler_params=params(),
            cost_estimate=cost(1, [v, x]),
        )(me, ranks, scales, v, x)

    def middle(arrived, route_in, route_out):
        shapes = shapes_sent(route_out, tiles, slots)
        result = pl.pallas_call(
            lambda *refs: middle_kernel(route_in, route_out, tiles, *refs),
            out_shape=[jax.ShapeDtypeStruct((2, height, 2 * n), jnp.bfloat16)] + shapes,
            in_specs=[SMEM, SMEM, SMEM, VMEM] + [VMEM] * len(arrived),
            out_specs=[VMEM] * (1 + len(shapes)),
            scratch_shapes=[pltpu.VMEM((2, tiles, width, 2 * n), jnp.bfloat16)],
            compiler_params=params(),
            cost_estimate=cost(2, [u, *arrived], 10),
        )(me, ranks, scales, u, *arrived)
        return result[0].reshape(2 * height, 2 * n), result[1:]

    def adjoint(arrived, route):
        return pl.pallas_call(
            lambda *refs: adjoint_kernel(route, tiles, *refs),
            out_shape=jax.ShapeDtypeStruct((height, 2 * n), jnp.bfloat16),
            in_specs=[SMEM, SMEM, VMEM] + [VMEM] * len(arrived),
            out_specs=VMEM,
            scratch_shapes=[pltpu.VMEM((tiles, 2 * width, 2 * n), jnp.bfloat16)],
            compiler_params=params(),
            cost_estimate=cost(1, [v, *arrived]),
        )(me, ranks, v, *arrived)

    def ordered(kernel, first, second, shape):
        return pl.pallas_call(
            kernel,
            out_shape=jax.ShapeDtypeStruct(shape, jnp.bfloat16),
            in_specs=[SMEM, VMEM, VMEM],
            out_specs=VMEM,
            compiler_params=params(),
        )(core_at, first, second)

    theirs = lax.dynamic_index_in_dim(wave_in, 1 - core, 0, keepdims=False)
    mine = lax.dynamic_index_in_dim(wave_in, core, 0, keepdims=False)
    other = lax.ppermute(theirs, "freq", swap)
    coded_a = code(other.reshape(height, 2 * n), way["1a"])
    first_a, sends_a = exchange(coded_a, way["1a"], tiles)
    (mine,) = after([mine], coded_a)
    first_b, sends_b = exchange(code(mine.reshape(height, 2 * n), way["1b"]), way["1b"], tiles)
    coded_a = second_hop(first_a, sends_a, way["1a"], tiles)
    coded_b = second_hop(first_b, sends_b, way["1b"], tiles)
    y_a, back_a = middle(coded_a, way["1a"], way["2a"])
    coded_b = after(coded_b, back_a)
    farthest_b = coded_b[way["1b"][0]]
    back_a = [*back_a[:2], *after(back_a[2:], [farthest_b])]
    first_a, sends_a = exchange(back_a, way["2a"], tiles)
    y_b, back_b = middle(coded_b, way["1b"], way["2b"])
    first_b, sends_b = exchange(back_b, way["2b"], tiles)
    back_a = second_hop(first_a, sends_a, way["2a"], tiles)
    back_b = second_hop(first_b, sends_b, way["2b"], tiles)
    z_a = lax.ppermute(adjoint(back_a, way["2a"]), "freq", swap)
    forward_out = ordered(order_rows_kernel, y_b, y_a, (2 * height, 4 * n))
    forward_out = forward_out.reshape(1, 2 * height, 2, 2 * n)
    z_b = adjoint(back_b, way["2b"])
    adjoint_out = ordered(order_parts_kernel, z_b, z_a, (2, height, 2 * n))
    return forward_out, adjoint_out.reshape(2, height, 2, n)


def solution(mesh):
    return jax.shard_map(
        per_device,
        mesh=mesh,
        in_specs=(
            P(None, "tile", None, "freq"),
            P("freq", None, "tile", None, None),
            P("freq", "tile", None, None, None),
            P("freq", None, None),
            P("freq", None, None),
        ),
        out_specs=(P("freq", "tile", None, None), P(None, "tile", None, "freq")),
        check_vma=False,
    )
```
